32 devices in a mesh: groups: 2 (over x), mesh: 8 (over z, y), inst: 2 (over core).
Axes of the slice: x: 2, y: 2, z: 4, core: 2. Of those that a mesh axis runs over, the one named last changes fastest.
Arguments:
- observations: bfloat16 [512, 128, 128], P(('groups', 'mesh', 'inst')), parts along dimension 0, may hold values from -6 to 6
- instrument: int32 [512], P(('groups', 'mesh', 'inst')), parts along dimension 0, may hold values from 0 to 3
- routes: int32 [512, 2], P(('groups', 'mesh', 'inst')), parts along dimension 0, may hold values from 0 to 7, all different within a row; in each aligned block of 16 rows (0 to 15, 16 to 31, ...) at most 8 rows name the same one
- offsets: int32 [512, 2], P(('groups', 'mesh', 'inst')), parts along dimension 0, may hold values from 0 to 1920
- edges: bfloat16 [512, 2, 128, 128], P(('groups', 'mesh', 'inst')), parts along dimension 0, may hold values from -0.1875 to 0.1875
- w_embed: bfloat16 [4, 128, 512], replicated, may hold values from -0.5 to 0.5
- w_mix: bfloat16 [512, 512], replicated, may hold values from -0.25 to 0.25
- w_node_in: bfloat16 [512, 512], replicated, may hold values from -0.25 to 0.25
- w_node_out: bfloat16 [512, 512], replicated, may hold values from -0.25 to 0.25
Outputs:
- latents: bfloat16 [32768, 512], P(('groups', 'mesh', 'inst')), parts along dimension 0
The draws below stay inside these ranges and needn't reach their ends.
There are 2 independent parts, one for each index of `groups`. The reference program is written for one: setup_inputs(seed, part) draws one part's arguments, and reference() takes and returns one part's arrays. A program takes and returns all parts, laid end to end along the dimension named above; an argument that names none is the same for every part. Nothing has to cross between parts.
Inputs may be any that keep to these rules, and one draw needn't show every extreme that they name: `routes`: each block names 2 different partitions; among the blocks of one device no partition is named more than 8 times, a bound that some block reaches.
All inputs are finite; a program needn't handle non-finite values.
Results may differ from the reference program's by a relative error of at most 0.0067.
Values may be sent and summed in bfloat16 or wider, within the bound.
A program may use at most 128 MiB of HBM per device.

```python
import math
import jax
import jax.numpy as jnp
import numpy as np
from jax import lax

D = 512
C_IN = 128
N_INSTR = 4
OBS = 128
TILE = 128
FP = 2
BLK_DEV = 16
NODE_PART = 2048
CAP = 8
BLOCKS = 256
NODES = 16384
N_MESH = 8
N_INST = 2


def place_ends(values, rng, least, largest):
    longest = values.shape.index(max(values.shape))
    spots = []
    for shift in (0, 1):
        where = [jax.random.randint(jax.random.fold_in(rng, axis), (), 0, length) for axis, length in enumerate(values.shape)]
        where[longest] = (where[longest] + shift) % values.shape[longest]
        spots.append(tuple(where))
    return values.at[spots[0]].set(least).at[spots[1]].set(largest)


def block_scale(rng, shape, split, low, high):
    level = 1.0
    for dim, shards_of in split:
        draws = jax.random.uniform(jax.random.fold_in(jax.random.fold_in(rng, 6), dim), (shards_of,), jnp.float32, low / len(split), high / len(split))
        level = level * jnp.repeat(jnp.exp(draws), shape[dim] // shards_of).reshape((-1,) + (1,) * (len(shape) - 1 - dim))
    return level


def shared_out(key, own, number, rows, number_of, top, most, slope):
    order = jax.random.permutation(key, number_of)
    packed, usual = shares(number_of, rows * top, most, slope, True), shares(number_of, rows * top, most, slope, False)
    places = jnp.arange(number_of)

    def named(lengths, rotation):
        used = int((lengths > 0).sum())
        fixed = max(1, used // 4)
        moved = fixed + (places - fixed + rotation * (used - fixed)) % max(1, number_of - fixed)
        return jnp.zeros((number_of,), jnp.int32).at[order[jnp.where(places < fixed, places, moved)]].set(jnp.asarray(lengths, jnp.int32))

    lengths = jnp.where(number % 4 == 0, named(packed, number // 4), named(usual, number - number // 4 - 1))
    mixed = jax.random.permutation(jax.random.fold_in(own, 3), number_of)
    donor, taker = mixed[0:number_of // 2 * 2:2], mixed[1:number_of // 2 * 2:2]
    slack = jnp.minimum(lengths[donor] - 1, most - lengths[taker]) // 2
    slack = jnp.where((donor == order[0]) | (taker == order[0]) | (lengths[taker] == 0), 0, jnp.maximum(slack, 0))
    moved = jax.random.randint(jax.random.fold_in(own, 4), (number_of // 2,), 0, 1 << 20) % (slack + 1)
    lengths = lengths.at[donor].add(-moved).at[taker].add(moved)
    items = jnp.searchsorted(jnp.cumsum(lengths), jnp.arange(rows * top), side="right").astype(jnp.int32)
    listing = items.reshape(top, rows).T
    listing = listing[jax.random.permutation(jax.random.fold_in(own, 1), rows)]
    rotation = jax.random.randint(jax.random.fold_in(own, 2), (rows, 1), 0, top)
    return jnp.take_along_axis(listing, (jnp.arange(top)[None, :] + rotation) % top, axis=1)


def shares(count, total, reach, skew, full):
    loads = [(1 << 20) // math.isqrt(grade ** skew) + 1 for grade in range(1, count + 1)]
    largest = reach if full else min(reach, max(-(-total // count), total * loads[0] // sum(loads)))
    least = 1 if total - largest >= count - 1 else 0
    counts, spare = [largest] + [least] * (count - 1), total - largest - least * (count - 1)
    while spare > 0:
        movable = [i for i in range(1, count) if counts[i] < largest] or [i for i in range(1, count) if counts[i] < reach]
        mass, left = sum([loads[i] for i in movable]), spare
        for i in movable:
            addition = min(reach - counts[i], max(1, left * loads[i] // mass), spare)
            counts[i] = counts[i] + addition
            spare = spare - addition
    return np.array(counts)


def normal_values(stream_key, shape, spread, reach, cuts=(), kind=jnp.bfloat16):
    drawn = jax.random.normal(stream_key, shape, jnp.float32) * spread
    if len(cuts) > 0:
        drawn = block_scale(stream_key, shape, cuts, -0.22, 0.18) * drawn
    return jnp.clip(drawn, min=-reach, max=reach).astype(kind)


def setup_inputs(seed: int = 0, part: int = 0) -> dict:
    splits = jax.random.split(jax.random.key(seed), 10)
    part_splits = jax.random.split(jax.random.fold_in(splits[9], part), 10)
    observations = normal_values(part_splits[0], (BLOCKS, OBS, C_IN), 1.0, 6.0, ((0, 16),))
    instrument = place_ends(jax.random.randint(part_splits[1], (BLOCKS,), 0, N_INSTR), jax.random.fold_in(part_splits[1], 1), 0, N_INSTR - 1).astype(jnp.int32)
    routes_keys = jax.random.split(jax.random.fold_in(part_splits[2], 1), BLOCKS // BLK_DEV)
    routes_turns = jax.random.permutation(jax.random.fold_in(part_splits[2], 3), BLOCKS // BLK_DEV)
    routes = jax.vmap(lambda own, number: shared_out(jax.random.fold_in(part_splits[2], 2), own, number, BLK_DEV, N_MESH, FP, CAP, 2))(routes_keys, routes_turns).reshape((BLOCKS, FP))
    offsets = place_ends(jax.random.randint(part_splits[3], (BLOCKS, FP), 0, NODE_PART - TILE + 1), jax.random.fold_in(part_splits[3], 1), 0, NODE_PART - TILE).astype(jnp.int32)
    edges = normal_values(part_splits[4], (BLOCKS, FP, OBS, TILE), (OBS * 8) ** -0.5, 0.1875, ((0, 16),))
    w_embed = normal_values(splits[5], (N_INSTR, C_IN, D), C_IN ** -0.5, 0.5)
    w_mix = normal_values(splits[6], (D, D), D ** -0.5, 0.25)
    w_node_in = normal_values(splits[7], (D, D), D ** -0.5, 0.25)
    w_node_out = normal_values(splits[8], (D, D), D ** -0.5, 0.25)
    return {"observations": observations, "instrument": instrument, "routes": routes, "offsets": offsets, "edges": edges, "w_embed": w_embed, "w_mix": w_mix, "w_node_in": w_node_in, "w_node_out": w_node_out}


def reference(observations, instrument, routes, offsets, edges, w_embed, w_mix, w_node_in, w_node_out):
    groups = N_MESH * N_INST
    obs_g = observations.reshape(groups, BLK_DEV, OBS, C_IN)
    ins_g = instrument.reshape(groups, BLK_DEV)
    rou_g = routes.reshape(groups, BLK_DEV, FP)
    off_g = offsets.reshape(groups, BLK_DEV, FP)
    edg_g = edges.reshape(groups, BLK_DEV, FP, OBS, TILE)
    mixer = w_mix.astype(jnp.float32)
    tile_rows = jnp.arange(TILE, dtype=jnp.int32)

    def step(summed, item):
        feats, kinds, dests, starts, weights = item
        chosen = jnp.take(w_embed, kinds, axis=0).astype(jnp.float32)
        first = jax.nn.silu(jnp.einsum('boc,bcd->bod', feats.astype(jnp.float32), chosen)).astype(jnp.bfloat16)
        embedded = jnp.einsum('bod,de->boe', first.astype(jnp.float32), mixer).astype(jnp.bfloat16)
        contrib = jnp.einsum('bjot,bod->bjtd', weights.astype(jnp.float32), embedded.astype(jnp.float32))
        rows = (dests * NODE_PART + starts).astype(jnp.int32)[:, :, None] + tile_rows[None, None, :]
        summed = summed.at[rows.reshape(-1)].add(contrib.reshape(-1, D))
        return (summed, None)
    summed, _ = lax.scan(step, jnp.zeros((NODES, D), jnp.float32), (obs_g, ins_g, rou_g, off_g, edg_g))
    normed = (summed * lax.rsqrt(lax.optimization_barrier(jnp.mean(summed * summed, axis=1, keepdims=True)) + 1e-06)).astype(jnp.bfloat16)
    inner = jax.nn.silu(jnp.dot(normed, w_node_in, preferred_element_type=jnp.float32)).astype(jnp.bfloat16)
    return (summed + jnp.dot(inner, w_node_out, preferred_element_type=jnp.float32)).astype(jnp.bfloat16)
```

```python
import functools

import jax
import jax.numpy as jnp
from jax import lax
from jax.experimental import pallas as pl
from jax.experimental.pallas import tpu as pltpu
from jax.sharding import PartitionSpec as P

NODE_PART = 2048
ANY = pl.ANY
VMEM = pltpu.VMEM
SMEM = pltpu.SMEM
MESH = pl.DeviceIdType.MESH
LIMIT = 48 * 1024 * 1024


def silu(v):
    return 0.5 * v * (1.0 + jnp.tanh(0.5 * v))


def pack_kernel(foot, source, obs, edges, out, sem):
    slots = out.shape[0]

    def step(s, carry):
        entry = source[s]
        pltpu.make_async_copy(obs.at[entry // foot], out.at[s, 0], sem).start()
        pltpu.make_async_copy(edges.at[entry], out.at[s, 1], sem).start()
        return carry

    lax.fori_loop(0, slots, step, 0)
    pltpu.make_async_copy(out, out, sem).wait()


def pack(source, obs, edges, foot):
    slots = source.shape[0]
    return pl.pallas_call(
        functools.partial(pack_kernel, foot),
        out_shape=jax.ShapeDtypeStruct((slots, 2) + obs.shape[1:], obs.dtype),
        in_specs=[
            pl.BlockSpec(memory_space=SMEM),
            pl.BlockSpec(memory_space=ANY),
            pl.BlockSpec(memory_space=ANY),
        ],
        out_specs=pl.BlockSpec(memory_space=ANY),
        scratch_shapes=[pltpu.SemaphoreType.DMA],
    )(source, obs, edges)


def tiles_kernel(first_chunk, last_chunk, meta, got, w_embed, *refs):
    if first_chunk:
        out, acc = refs
        acc[...] = jnp.zeros_like(acc)
    else:
        held, out, acc = refs
        acc[:NODE_PART, :] = held[...]
    slots = got.shape[0]

    def step(s, carry):
        word = meta[s]

        @pl.when(word >= 8192)
        def _():
            kind = (word // 2048) % 4
            start = word % 2048
            v = jnp.dot(got[s, 0], w_embed[kind], preferred_element_type=jnp.float32)
            first = silu(v).astype(jnp.bfloat16)
            turn = start % 8
            base = pl.multiple_of(start - turn, 8)
            turned = pltpu.roll(got[s, 1].astype(jnp.float32), turn, 1).astype(jnp.bfloat16)
            term = lax.dot_general(
                turned, first, (((0,), (0,)), ((), ())), preferred_element_type=jnp.float32
            )
            tile_n = term.shape[0]
            head = term[:8]
            low = lax.broadcasted_iota(jnp.int32, head.shape, 0) < turn
            acc[pl.ds(base, 8), :] += jnp.where(low, 0.0, head)
            acc[pl.ds(base + 8, tile_n - 8), :] += term[8:]
            acc[pl.ds(base + tile_n, 8), :] += jnp.where(low, head, 0.0)

        return carry

    lax.fori_loop(0, slots, step, 0)
    out[...] = acc[:NODE_PART, :].astype(out.dtype)


def tiles(meta, got, w_embed, held, last_chunk):
    width = w_embed.shape[2]
    args = [meta, got, w_embed] + ([] if held is None else [held])
    return pl.pallas_call(
        functools.partial(tiles_kernel, held is None, last_chunk),
        out_shape=jax.ShapeDtypeStruct(
            (NODE_PART, width), jnp.bfloat16 if last_chunk else jnp.float32
        ),
        in_specs=[pl.BlockSpec(memory_space=SMEM)]
        + [pl.BlockSpec(memory_space=VMEM)] * (len(args) - 1),
        out_specs=pl.BlockSpec(memory_space=VMEM),
        scratch_shapes=[pltpu.VMEM((NODE_PART + 8, width), jnp.float32)],
        compiler_params=pltpu.CompilerParams(vmem_limit_bytes=LIMIT),
    )(*args)


def nodes_kernel(pieces, own_sums, w_mix, w_in, w_out, out, got, send_sem, recv_sem):
    me = lax.axis_index("inst")
    other = 1 - me
    half = out.shape[0]
    rows = half // pieces
    barrier = pltpu.get_barrier_semaphore()
    pl.semaphore_signal(barrier, inc=1, device_id={"inst": other}, device_id_type=MESH)
    pl.semaphore_wait(barrier, 1)
    copies = []
    for i in range(pieces):
        copy = pltpu.make_async_remote_copy(
            src_ref=own_sums.at[pl.ds(pl.multiple_of(other * half + i * rows, rows), rows)],
            dst_ref=got.at[pl.ds(i * rows, rows)],
            send_sem=send_sem.at[i],
            recv_sem=recv_sem.at[i],
            device_id={"inst": other},
            device_id_type=MESH,
        )
        copy.start()
        copies.append(copy)
    for i in range(pieces):
        copies[i].wait_recv()
        mine = own_sums[pl.ds(pl.multiple_of(me * half + i * rows, rows), rows), :]
        total = mine.astype(jnp.float32) + got[pl.ds(i * rows, rows), :].astype(jnp.float32)
        summed = jnp.dot(
            total.astype(jnp.bfloat16), w_mix[...], preferred_element_type=jnp.float32
        )
        scale = lax.rsqrt(jnp.mean(summed * summed, axis=1, keepdims=True) + 1e-06)
        normed = (summed * scale).astype(jnp.bfloat16)
        inner = silu(jnp.dot(normed, w_in[...], preferred_element_type=jnp.float32))
        out[pl.ds(i * rows, rows), :] = (
            summed
            + jnp.dot(inner.astype(jnp.bfloat16), w_out[...], preferred_element_type=jnp.float32)
        ).astype(out.dtype)
    for i in range(pieces):
        copies[i].wait_send()


def nodes(own_sums, w_mix, w_in, w_out, n_inst):
    total, width = own_sums.shape
    half = total // n_inst
    pieces = 4
    return pl.pallas_call(
        functools.partial(nodes_kernel, pieces),
        out_shape=jax.ShapeDtypeStruct((half, width), jnp.bfloat16),
        in_specs=[pl.BlockSpec(memory_space=VMEM)] * 4,
        out_specs=pl.BlockSpec(memory_space=VMEM),
        scratch_shapes=[
            pltpu.VMEM((half, width), jnp.bfloat16),
            pltpu.SemaphoreType.DMA((pieces,)),
            pltpu.SemaphoreType.DMA((pieces,)),
        ],
        compiler_params=pltpu.CompilerParams(
            collective_id=0, has_side_effects=True, vmem_limit_bytes=LIMIT
        ),
    )(own_sums, w_mix, w_in, w_out)


def per_device(
    observations, instrument, routes, offsets, edges, w_embed, w_mix, w_node_in, w_node_out
):
    n_mesh = lax.axis_size("mesh")
    n_inst = lax.axis_size("inst")
    blocks, obs_n, feats = observations.shape
    foot = routes.shape[1]
    tile_n = edges.shape[3]
    cap = max(2, 2 * blocks * foot // n_mesh)
    chunks = 1
    per = cap // chunks
    slots = n_mesh * cap
    entries = blocks * foot
    dest = routes.reshape(entries)
    index = jnp.arange(entries, dtype=jnp.int32)
    same = (dest[:, None] == dest[None, :]) & (index[None, :] < index[:, None])
    rank = jnp.sum(same.astype(jnp.int32), axis=1)
    position = (rank // per) * (n_mesh * per) + dest * per + rank % per
    words = offsets.reshape(entries) + 2048 * jnp.repeat(instrument, foot) + 8192
    hit = position[None, :] == jnp.arange(slots, dtype=jnp.int32)[:, None]
    source = jnp.sum(jnp.where(hit, index[None, :], 0), axis=1)
    meta = jnp.sum(jnp.where(hit, words[None, :], 0), axis=1)
    got_meta = lax.all_to_all(
        meta.reshape(chunks, n_mesh, per), "mesh", split_axis=1, concat_axis=1, tiled=True
    ).reshape(chunks, n_mesh * per)
    packed = pack(source, observations, edges.reshape(entries, obs_n, tile_n), foot)
    packed = packed.reshape((chunks, n_mesh, per) + packed.shape[1:])
    held = None
    for k in range(chunks):
        got = lax.all_to_all(packed[k], "mesh", split_axis=0, concat_axis=0, tiled=True)
        got = got.reshape((n_mesh * per,) + got.shape[2:])
        held = tiles(got_meta[k], got, w_embed, held, k == chunks - 1)
    return nodes(held, w_mix, w_node_in, w_node_out, n_inst)


def solution(mesh):
    return jax.shard_map(
        per_device,
        mesh=mesh,
        in_specs=(
            P(("groups", "mesh", "inst"), None, None),
            P(("groups", "mesh", "inst")),
            P(("groups", "mesh", "inst"), None),
            P(("groups", "mesh", "inst"), None),
            P(("groups", "mesh", "inst"), None, None, None),
            P(),
            P(),
            P(),
            P(),
        ),
        out_specs=P(("groups", "mesh", "inst"), None),
        check_vma=False,
    )
```

```python
import functools

import jax
import jax.numpy as jnp
from jax import lax
from jax.experimental import pallas as pl
from jax.experimental.pallas import tpu as pltpu
from jax.sharding import PartitionSpec as P

NODE_PART = 2048
ANY = pl.ANY
VMEM = pltpu.VMEM
SMEM = pltpu.SMEM
MESH = pl.DeviceIdType.MESH
LIMIT = 48 * 1024 * 1024


def silu(v):
    return 0.5 * v * (1.0 + jnp.tanh(0.5 * v))


def pack_kernel(foot, source, obs, edges, out, sem):
    slots = out.shape[0]

    def step(s, carry):
        entry = source[s]
        pltpu.make_async_copy(obs.at[entry // foot], out.at[s, 0], sem).start()
        pltpu.make_async_copy(edges.at[entry], out.at[s, 1], sem).start()
        return carry

    lax.fori_loop(0, slots, step, 0)
    pltpu.make_async_copy(out, out, sem).wait()


def pack(source, obs, edges, foot):
    slots = source.shape[0]
    return pl.pallas_call(
        functools.partial(pack_kernel, foot),
        out_shape=jax.ShapeDtypeStruct((slots, 2) + obs.shape[1:], obs.dtype),
        in_specs=[
            pl.BlockSpec(memory_space=SMEM),
            pl.BlockSpec(memory_space=VMEM),
            pl.BlockSpec(memory_space=VMEM),
        ],
        out_specs=pl.BlockSpec(memory_space=ANY),
        scratch_shapes=[pltpu.SemaphoreType.DMA],
        compiler_params=pltpu.CompilerParams(vmem_limit_bytes=LIMIT),
    )(source, obs, edges)


def tiles_kernel(first_chunk, last_chunk, meta, got, w_embed, *refs):
    if first_chunk:
        out, acc = refs
        acc[...] = jnp.zeros_like(acc)
    else:
        held, out, acc = refs
        acc[:NODE_PART, :] = held[...]
    slots = got.shape[0]

    def step(s, carry):
        word = meta[s]

        @pl.when(word >= 8192)
        def _():
            kind = (word // 2048) % 4
            start = word % 2048
            v = jnp.dot(got[s, 0], w_embed[kind], preferred_element_type=jnp.float32)
            first = silu(v).astype(jnp.bfloat16)
            turn = start % 8
            base = pl.multiple_of(start - turn, 8)
            turned = pltpu.roll(got[s, 1].astype(jnp.float32), turn, 1).astype(jnp.bfloat16)
            term = lax.dot_general(
                turned, first, (((0,), (0,)), ((), ())), preferred_element_type=jnp.float32
            )
            tile_n = term.shape[0]
            head = term[:8]
            low = lax.broadcasted_iota(jnp.int32, head.shape, 0) < turn
            acc[pl.ds(base, 8), :] += jnp.where(low, 0.0, head)
            acc[pl.ds(base + 8, tile_n - 8), :] += term[8:]
            acc[pl.ds(base + tile_n, 8), :] += jnp.where(low, head, 0.0)

        return carry

    lax.fori_loop(0, slots, step, 0)
    out[...] = acc[:NODE_PART, :].astype(out.dtype)


def tiles(meta, got, w_embed, held, last_chunk):
    width = w_embed.shape[2]
    args = [meta, got, w_embed] + ([] if held is None else [held])
    return pl.pallas_call(
        functools.partial(tiles_kernel, held is None, last_chunk),
        out_shape=jax.ShapeDtypeStruct(
            (NODE_PART, width), jnp.bfloat16 if last_chunk else jnp.float32
        ),
        in_specs=[pl.BlockSpec(memory_space=SMEM)]
        + [pl.BlockSpec(memory_space=VMEM)] * (len(args) - 1),
        out_specs=pl.BlockSpec(memory_space=VMEM),
        scratch_shapes=[pltpu.VMEM((NODE_PART + 8, width), jnp.float32)],
        compiler_params=pltpu.CompilerParams(vmem_limit_bytes=LIMIT),
    )(*args)


def nodes_kernel(pieces, own_sums, w_mix, w_in, w_out, out, got, send_sem, recv_sem):
    me = lax.axis_index("inst")
    other = 1 - me
    half = out.shape[0]
    rows = half // pieces
    barrier = pltpu.get_barrier_semaphore()
    pl.semaphore_signal(barrier, inc=1, device_id={"inst": other}, device_id_type=MESH)
    pl.semaphore_wait(barrier, 1)
    copies = []
    for i in range(pieces):
        copy = pltpu.make_async_remote_copy(
            src_ref=own_sums.at[pl.ds(pl.multiple_of(other * half + i * rows, rows), rows)],
            dst_ref=got.at[pl.ds(i * rows, rows)],
            send_sem=send_sem.at[i],
            recv_sem=recv_sem.at[i],
            device_id={"inst": other},
            device_id_type=MESH,
        )
        copy.start()
        copies.append(copy)
    for i in range(pieces):
        copies[i].wait_recv()
        mine = own_sums[pl.ds(pl.multiple_of(me * half + i * rows, rows), rows), :]
        total = mine.astype(jnp.float32) + got[pl.ds(i * rows, rows), :].astype(jnp.float32)
        summed = jnp.dot(
            total.astype(jnp.bfloat16), w_mix[...], preferred_element_type=jnp.float32
        )
        scale = lax.rsqrt(jnp.mean(summed * summed, axis=1, keepdims=True) + 1e-06)
        normed = (summed * scale).astype(jnp.bfloat16)
        inner = silu(jnp.dot(normed, w_in[...], preferred_element_type=jnp.float32))
        out[pl.ds(i * rows, rows), :] = (
            summed
            + jnp.dot(inner.astype(jnp.bfloat16), w_out[...], preferred_element_type=jnp.float32)
        ).astype(out.dtype)
    for i in range(pieces):
        copies[i].wait_send()


def nodes(own_sums, w_mix, w_in, w_out, n_inst):
    total, width = own_sums.shape
    half = total // n_inst
    pieces = 4
    return pl.pallas_call(
        functools.partial(nodes_kernel, pieces),
        out_shape=jax.ShapeDtypeStruct((half, width), jnp.bfloat16),
        in_specs=[pl.BlockSpec(memory_space=VMEM)] * 4,
        out_specs=pl.BlockSpec(memory_space=VMEM),
        scratch_shapes=[
            pltpu.VMEM((half, width), jnp.bfloat16),
            pltpu.SemaphoreType.DMA((pieces,)),
            pltpu.SemaphoreType.DMA((pieces,)),
        ],
        compiler_params=pltpu.CompilerParams(
            collective_id=0, has_side_effects=True, vmem_limit_bytes=LIMIT
        ),
    )(own_sums, w_mix, w_in, w_out)


def per_device(
    observations, instrument, routes, offsets, edges, w_embed, w_mix, w_node_in, w_node_out
):
    n_mesh = lax.axis_size("mesh")
    n_inst = lax.axis_size("inst")
    blocks, obs_n, feats = observations.shape
    foot = routes.shape[1]
    tile_n = edges.shape[3]
    cap = max(2, 2 * blocks * foot // n_mesh)
    chunks = min(2, cap)
    per = cap // chunks
    slots = n_mesh * cap
    entries = blocks * foot
    dest = routes.reshape(entries)
    index = jnp.arange(entries, dtype=jnp.int32)
    same = (dest[:, None] == dest[None, :]) & (index[None, :] < index[:, None])
    rank = jnp.sum(same.astype(jnp.int32), axis=1)
    position = (rank // per) * (n_mesh * per) + dest * per + rank % per
    words = offsets.reshape(entries) + 2048 * jnp.repeat(instrument, foot) + 8192
    hit = position[None, :] == jnp.arange(slots, dtype=jnp.int32)[:, None]
    source = jnp.sum(jnp.where(hit, index[None, :], 0), axis=1)
    meta = jnp.sum(jnp.where(hit, words[None, :], 0), axis=1)
    got_meta = lax.all_to_all(
        meta.reshape(chunks, n_mesh, per), "mesh", split_axis=1, concat_axis=1, tiled=True
    ).reshape(chunks, n_mesh * per)
    packed = pack(source, observations, edges.reshape(entries, obs_n, tile_n), foot)
    packed = packed.reshape((chunks, n_mesh, per) + packed.shape[1:])
    held = None
    for k in range(chunks):
        got = lax.all_to_all(packed[k], "mesh", split_axis=0, concat_axis=0, tiled=True)
        got = got.reshape((n_mesh * per,) + got.shape[2:])
        held = tiles(got_meta[k], got, w_embed, held, k == chunks - 1)
    return nodes(held, w_mix, w_node_in, w_node_out, n_inst)


def solution(mesh):
    return jax.shard_map(
        per_device,
        mesh=mesh,
        in_specs=(
            P(("groups", "mesh", "inst"), None, None),
            P(("groups", "mesh", "inst")),
            P(("groups", "mesh", "inst"), None),
            P(("groups", "mesh", "inst"), None),
            P(("groups", "mesh", "inst"), None, None, None),
            P(),
            P(),
            P(),
            P(),
        ),
        out_specs=P(("groups", "mesh", "inst"), None),
        check_vma=False,
    )
```

```python
import functools

import jax
import jax.numpy as jnp
from jax import lax
from jax.experimental import pallas as pl
from jax.experimental.pallas import tpu as pltpu
from jax.sharding import PartitionSpec as P

NODE_PART = 2048
ANY = pl.ANY
VMEM = pltpu.VMEM
SMEM = pltpu.SMEM
MESH = pl.DeviceIdType.MESH
LIMIT = 48 * 1024 * 1024


def silu(v):
    return 0.5 * v * (1.0 + jnp.tanh(0.5 * v))


def pack_kernel(foot, source, meta, obs, edges, out):
    tile_n = edges.shape[2]

    def step(s, carry):
        entry = source[s]
        out[s, 0] = obs[entry // foot]
        nodes_first = edges[entry].astype(jnp.float32).T
        out[s, 1] = pltpu.roll(nodes_first, meta[s] % tile_n, 0).astype(out.dtype)
        return carry

    lax.fori_loop(0, out.shape[0], step, 0)


def pack(source, meta, obs, edges, foot):
    slots = source.shape[0]
    return pl.pallas_call(
        functools.partial(pack_kernel, foot),
        out_shape=jax.ShapeDtypeStruct((slots, 2) + obs.shape[1:], obs.dtype),
        in_specs=[pl.BlockSpec(memory_space=SMEM)] * 2 + [pl.BlockSpec(memory_space=VMEM)] * 2,
        out_specs=pl.BlockSpec(memory_space=VMEM),
        compiler_params=pltpu.CompilerParams(vmem_limit_bytes=LIMIT),
    )(source, meta, obs, edges)


def main_kernel(
    packed, words, w_embed, w_mix, w_in, w_out, out,
    got, got_words, acc, kinds_obs, first, placed, leaving, arrived,
    send_sem, recv_sem, word_send, word_recv, half_send, half_recv,
):
    cap, n_mesh = got.shape[0], got.shape[1]
    tile_n, feats = got.shape[3], got.shape[4]
    n_kinds = w_embed.shape[0] // feats
    unit = kinds_obs.shape[0] // tile_n
    groups = n_mesh // unit
    half = out.shape[0]
    pieces = half_send.shape[0]
    rows = half // pieces
    me = lax.axis_index("mesh")
    core = lax.axis_index("inst")
    other = 1 - core

    barrier = pltpu.get_barrier_semaphore()

    def greet(i, carry):
        to = lax.rem(me + i, n_mesh)
        pl.semaphore_signal(barrier, inc=1, device_id={"mesh": to}, device_id_type=MESH)
        return carry

    lax.fori_loop(1, n_mesh, greet, 0)
    pl.semaphore_signal(barrier, inc=1, device_id={"inst": other}, device_id_type=MESH)

    def own(j):
        return pltpu.make_async_copy(packed.at[j, me], got.at[j, me], recv_sem.at[j, me])

    def own_words():
        return pltpu.make_async_copy(words.at[me], got_words.at[me], word_recv.at[me])

    def start_own(j, carry):
        own(j).start()
        return carry

    own_words().start()
    lax.fori_loop(0, cap, start_own, 0)
    acc[...] = jnp.zeros_like(acc)
    pl.semaphore_wait(barrier, n_mesh)

    def entry_copy(j, to):
        return pltpu.make_async_remote_copy(
            src_ref=packed.at[j, to],
            dst_ref=got.at[j, me],
            send_sem=send_sem.at[j, to],
            recv_sem=recv_sem.at[j, me],
            device_id={"mesh": to},
            device_id_type=MESH,
        )

    def word_copy(to):
        return pltpu.make_async_remote_copy(
            src_ref=words.at[to],
            dst_ref=got_words.at[me],
            send_sem=word_send.at[to],
            recv_sem=word_recv.at[me],
            device_id={"mesh": to},
            device_id_type=MESH,
        )

    def start_words(i, carry):
        word_copy(lax.rem(me + i, n_mesh)).start()
        return carry

    lax.fori_loop(1, n_mesh, start_words, 0)

    def start_rank(j, carry):
        def start_one(i, c):
            entry_copy(j, lax.rem(me + i, n_mesh)).start()
            return c

        return lax.fori_loop(1, n_mesh, start_one, carry)

    lax.fori_loop(0, cap, start_rank, 0)

    def wait_words(s, carry):
        pltpu.make_async_copy(words.at[s], got_words.at[s], word_recv.at[s]).wait()
        return carry

    lax.fori_loop(0, n_mesh, wait_words, 0)

    place = lax.broadcasted_iota(jnp.int32, (tile_n, tile_n), 0)
    group_rows = placed.shape[0]
    tiles = group_rows // tile_n

    def work(u, carry):
        j = u // groups
        base = (u % groups) * unit
        owners = []
        for s in range(unit):
            src = base + s
            pltpu.make_async_copy(packed.at[j, src], got.at[j, src], recv_sem.at[j, src]).wait()
            word = got_words[src, pl.ds(j, 1), :]
            kind = (word // NODE_PART) % 4
            x = got[j, src, 0]
            for k in range(n_kinds):
                mask = jnp.broadcast_to((kind == k).astype(jnp.float32), (tile_n, feats))
                kinds_obs[s * tile_n : (s + 1) * tile_n, k * feats : (k + 1) * feats] = (
                    x * mask.astype(jnp.bfloat16)
                )
            begin = word % NODE_PART
            q = jnp.where(word >= 4 * NODE_PART, begin // tile_n, -100)
            owner = q + jnp.where(place < begin % tile_n, 1, 0)
            owners.append(owner.astype(jnp.float32).astype(jnp.bfloat16))
        first[...] = silu(
            jnp.dot(kinds_obs[...], w_embed[...], preferred_element_type=jnp.float32)
        ).astype(jnp.bfloat16)
        for g in range(NODE_PART // group_rows):
            for s in range(unit):
                weights = got[j, base + s, 1]
                for n in range(tiles):
                    here = owners[s] == jnp.bfloat16(g * tiles + n)
                    placed[n * tile_n : (n + 1) * tile_n, s * tile_n : (s + 1) * tile_n] = (
                        jnp.where(here, weights, jnp.bfloat16(0))
                    )
            acc[g * group_rows : (g + 1) * group_rows, :] += jnp.dot(
                placed[...], first[...], preferred_element_type=jnp.float32
            )
        return carry

    lax.fori_loop(0, cap * groups, work, 0)

    def half_copy(i):
        return pltpu.make_async_remote_copy(
            src_ref=leaving.at[pl.ds(i * rows, rows)],
            dst_ref=arrived.at[pl.ds(i * rows, rows)],
            send_sem=half_send.at[i],
            recv_sem=half_recv.at[i],
            device_id={"inst": other},
            device_id_type=MESH,
        )

    for i in range(pieces):
        theirs = acc[pl.ds(pl.multiple_of(other * half + i * rows, rows), rows), :]
        leaving[pl.ds(i * rows, rows), :] = theirs.astype(jnp.bfloat16)
        half_copy(i).start()
    for i in range(pieces):
        half_copy(i).wait_recv()
        mine = acc[pl.ds(pl.multiple_of(core * half + i * rows, rows), rows), :]
        total = mine + arrived[pl.ds(i * rows, rows), :].astype(jnp.float32)
        summed = jnp.dot(
            total.astype(jnp.bfloat16), w_mix[...], preferred_element_type=jnp.float32
        )
        scale = lax.rsqrt(jnp.mean(summed * summed, axis=1, keepdims=True) + 1e-06)
        normed = (summed * scale).astype(jnp.bfloat16)
        inner = silu(jnp.dot(normed, w_in[...], preferred_element_type=jnp.float32))
        out[pl.ds(i * rows, rows), :] = (
            summed
            + jnp.dot(inner.astype(jnp.bfloat16), w_out[...], preferred_element_type=jnp.float32)
        ).astype(out.dtype)
    for i in range(pieces):
        half_copy(i).wait_send()

    def end_rank(j, carry):
        def end_one(i, c):
            entry_copy(j, lax.rem(me + i, n_mesh)).wait_send()
            return c

        return lax.fori_loop(1, n_mesh, end_one, carry)

    def end_words(i, carry):
        word_copy(lax.rem(me + i, n_mesh)).wait_send()
        return carry

    lax.fori_loop(0, cap, end_rank, 0)
    lax.fori_loop(1, n_mesh, end_words, 0)


def main(packed, words, w_embed, w_mix, w_in, w_out, n_inst):
    cap, n_mesh, _, obs_n, feats = packed.shape
    width = w_mix.shape[0]
    half = NODE_PART // n_inst
    unit = min(8, n_mesh)
    pieces = 4
    bf16 = jnp.bfloat16
    return pl.pallas_call(
        main_kernel,
        out_shape=jax.ShapeDtypeStruct((half, width), bf16),
        in_specs=[pl.BlockSpec(memory_space=VMEM)] * 6,
        out_specs=pl.BlockSpec(memory_space=VMEM),
        scratch_shapes=[
            pltpu.VMEM(packed.shape, bf16),
            pltpu.VMEM(words.shape, jnp.int32),
            pltpu.VMEM((NODE_PART, width), jnp.float32),
            pltpu.VMEM((unit * obs_n, w_embed.shape[0]), bf16),
            pltpu.VMEM((unit * obs_n, width), bf16),
            pltpu.VMEM((512, unit * obs_n), bf16),
            pltpu.VMEM((half, width), bf16),
            pltpu.VMEM((half, width), bf16),
            pltpu.SemaphoreType.DMA((cap, n_mesh)),
            pltpu.SemaphoreType.DMA((cap, n_mesh)),
            pltpu.SemaphoreType.DMA((n_mesh,)),
            pltpu.SemaphoreType.DMA((n_mesh,)),
            pltpu.SemaphoreType.DMA((pieces,)),
            pltpu.SemaphoreType.DMA((pieces,)),
        ],
        compiler_params=pltpu.CompilerParams(
            collective_id=0, has_side_effects=True, vmem_limit_bytes=LIMIT
        ),
    )(packed, words, w_embed, w_mix, w_in, w_out)


def per_device(
    observations, instrument, routes, offsets, edges, w_embed, w_mix, w_node_in, w_node_out
):
    n_mesh = lax.axis_size("mesh")
    n_inst = lax.axis_size("inst")
    blocks, obs_n, feats = observations.shape
    foot = routes.shape[1]
    tile_n = edges.shape[3]
    cap = max(2, 2 * blocks * foot // n_mesh)
    slots = n_mesh * cap
    entries = blocks * foot
    dest = routes.reshape(entries)
    index = jnp.arange(entries, dtype=jnp.int32)
    same = (dest[:, None] == dest[None, :]) & (index[None, :] < index[:, None])
    rank = jnp.sum(same.astype(jnp.int32), axis=1)
    position = rank * n_mesh + dest
    words = offsets.reshape(entries) + NODE_PART * jnp.repeat(instrument, foot) + 4 * NODE_PART
    hit = position[None, :] == jnp.arange(slots, dtype=jnp.int32)[:, None]
    source = jnp.sum(jnp.where(hit, index[None, :], 0), axis=1)
    meta = jnp.sum(jnp.where(hit, words[None, :], 0), axis=1)
    packed = pack(source, meta, observations, edges.reshape(entries, obs_n, tile_n), foot)
    packed = packed.reshape((cap, n_mesh) + packed.shape[1:])
    by_dest = jnp.pad(meta.reshape(cap, n_mesh).T, ((0, 0), (0, max(8, cap) - cap)))
    spread = jnp.broadcast_to(by_dest[:, :, None], by_dest.shape + (feats,))
    return main(
        packed, spread, w_embed.reshape(-1, w_embed.shape[2]), w_mix, w_node_in, w_node_out, n_inst
    )


def solution(mesh):
    return jax.shard_map(
        per_device,
        mesh=mesh,
        in_specs=(
            P(("groups", "mesh", "inst"), None, None),
            P(("groups", "mesh", "inst")),
            P(("groups", "mesh", "inst"), None),
            P(("groups", "mesh", "inst"), None),
            P(("groups", "mesh", "inst"), None, None, None),
            P(),
            P(),
            P(),
            P(),
        ),
        out_specs=P(("groups", "mesh", "inst"), None),
        check_vma=False,
    )
```

```python
import functools

import jax
import jax.numpy as jnp
from jax import lax
from jax.experimental import pallas as pl
from jax.experimental.pallas import tpu as pltpu
from jax.sharding import PartitionSpec as P

NODE_PART = 2048
ANY = pl.ANY
VMEM = pltpu.VMEM
SMEM = pltpu.SMEM
MESH = pl.DeviceIdType.MESH
LIMIT = 48 * 1024 * 1024
RELAY = True


def silu(v):
    return 0.5 * v * (1.0 + jnp.tanh(0.5 * v))


def main_kernel(
    relay, foot, source, obs, edges, words, w_embed, w_mix, w_in, w_out, out,
    packed, got, got_words, acc, kinds_obs, first, placed, leaving, arrived,
    far_leaving, far_arrived, dense_out, dense_in,
    send_sem, recv_sem, word_send, word_recv, half_send, half_recv,
    far_send, far_recv, dense_send, dense_recv,
):
    parts, cap, n_part = got.shape[0], got.shape[1], got.shape[2]
    n_mesh = parts * n_part
    tile_n, feats = got.shape[4], got.shape[5]
    n_kinds = w_embed.shape[0] // feats
    unit = kinds_obs.shape[0] // tile_n
    half = out.shape[0]
    pieces = half_send.shape[0]
    rows = half // pieces
    me = lax.axis_index("mesh")
    part = me // n_part
    place_in = lax.rem(me, n_part)
    across = lax.rem(me + n_part, n_mesh)
    core = lax.axis_index("inst")
    other = 1 - core

    def device(k):
        return part * n_part + k

    def dest(f, k):
        return lax.rem(part + parts - 1 - f, parts) * n_part + k

    barrier = pltpu.get_barrier_semaphore()

    def greet(t, carry):
        to = device(lax.rem(place_in + t, n_part))
        pl.semaphore_signal(barrier, inc=1, device_id={"mesh": to}, device_id_type=MESH)
        return carry

    lax.fori_loop(1, n_part, greet, 0)
    if relay:
        pl.semaphore_signal(barrier, inc=1, device_id={"mesh": across}, device_id_type=MESH)
    pl.semaphore_signal(barrier, inc=1, device_id={"inst": other}, device_id_type=MESH)

    def pack(f, j):
        def one(k, carry):
            entry = source[j * n_mesh + dest(f, k)]
            packed[f, j, k, 0] = obs[entry // foot]
            packed[f, j, k, 1] = edges[entry]
            return carry

        lax.fori_loop(0, n_part, one, 0)

    def entry_copy(f, j, k):
        return pltpu.make_async_remote_copy(
            src_ref=packed.at[f, j, k],
            dst_ref=got.at[f, j, place_in],
            send_sem=send_sem.at[f, j, k],
            recv_sem=recv_sem.at[f, j, place_in],
            device_id={"mesh": device(k)},
            device_id_type=MESH,
        )

    def word_copy(f, k):
        return pltpu.make_async_remote_copy(
            src_ref=words.at[dest(f, k)],
            dst_ref=got_words.at[f, place_in],
            send_sem=word_send.at[f, k],
            recv_sem=word_recv.at[f, place_in],
            device_id={"mesh": device(k)},
            device_id_type=MESH,
        )

    pack(0, 0)
    pl.semaphore_wait(barrier, n_part + (1 if relay else 0))
    for f in range(parts):
        pltpu.make_async_copy(
            words.at[dest(f, place_in)], got_words.at[f, place_in], word_recv.at[f, place_in]
        ).start()

        def start_word(t, carry):
            word_copy(f, lax.rem(place_in + t, n_part)).start()
            return carry

        lax.fori_loop(1, n_part, start_word, 0)

    for f in range(parts):

        def start_rank(j, carry):
            if f == 0:

                @pl.when(j > 0)
                def _():
                    pack(f, j)

            else:
                pack(f, j)
            pltpu.make_async_copy(
                packed.at[f, j, place_in], got.at[f, j, place_in], recv_sem.at[f, j, place_in]
            ).start()

            def start_one(t, c):
                entry_copy(f, j, lax.rem(place_in + t, n_part)).start()
                return c

            return lax.fori_loop(1, n_part, start_one, carry)

        lax.fori_loop(0, cap, start_rank, 0)

    for f in range(parts):

        def wait_word(s, carry):
            pltpu.make_async_copy(words.at[s], got_words.at[f, s], word_recv.at[f, s]).wait()
            return carry

        lax.fori_loop(0, n_part, wait_word, 0)

    place = lax.broadcasted_iota(jnp.int32, (tile_n, tile_n), 0)
    lane = lax.broadcasted_iota(jnp.int32, (tile_n, tile_n), 1)
    group_rows = placed.shape[0]
    tiles = group_rows // tile_n

    def sums(f):
        acc[...] = jnp.zeros_like(acc)

        def work(u, carry):
            owners = []
            turned = []
            for s in range(unit):
                slot = u * unit + s
                j = slot // n_part
                src = lax.rem(slot, n_part)
                pltpu.make_async_copy(
                    packed.at[f, j, src], got.at[f, j, src], recv_sem.at[f, j, src]
                ).wait()
                word = got_words[f, src, pl.ds(j, 1), :]
                kind = (word // NODE_PART) % 4
                x = got[f, j, src, 0]
                for k in range(n_kinds):
                    mask = jnp.broadcast_to((kind == k).astype(jnp.float32), (tile_n, feats))
                    kinds_obs[s * tile_n : (s + 1) * tile_n, k * feats : (k + 1) * feats] = (
                        x * mask.astype(jnp.bfloat16)
                    )
                begin = word % NODE_PART
                turn = begin % tile_n
                q = jnp.where(word >= 4 * NODE_PART, begin // tile_n, -100)
                owner = q + jnp.where(place < turn, 1, 0)
                owners.append(owner.astype(jnp.float32).astype(jnp.bfloat16))
                moves = jnp.where((lane + turn) % tile_n == place, 1.0, 0.0).astype(jnp.bfloat16)
                turned.append(
                    lax.dot_general(
                        moves, got[f, j, src, 1], (((1,), (1,)), ((), ())),
                        preferred_element_type=jnp.float32,
                    ).astype(jnp.bfloat16)
                )
            first[...] = silu(
                jnp.dot(kinds_obs[...], w_embed[...], preferred_element_type=jnp.float32)
            ).astype(jnp.bfloat16)
            for g in range(NODE_PART // group_rows):
                for s in range(unit):
                    for n in range(tiles):
                        here = owners[s] == jnp.bfloat16(g * tiles + n)
                        placed[n * tile_n : (n + 1) * tile_n, s * tile_n : (s + 1) * tile_n] = (
                            jnp.where(here, turned[s], jnp.bfloat16(0))
                        )
                acc[g * group_rows : (g + 1) * group_rows, :] += jnp.dot(
                    placed[...], first[...], preferred_element_type=jnp.float32
                )
            return carry

        lax.fori_loop(0, cap * n_part // unit, work, 0)

    def to_core(src, dst, sent, come, i):
        return pltpu.make_async_remote_copy(
            src_ref=src.at[pl.ds(i * rows, rows)],
            dst_ref=dst.at[pl.ds(i * rows, rows)],
            send_sem=sent.at[i],
            recv_sem=come.at[i],
            device_id={"inst": other},
            device_id_type=MESH,
        )

    def far_copy(i):
        return to_core(far_leaving, far_arrived, far_send, far_recv, i)

    def half_copy(i):
        return to_core(leaving, arrived, half_send, half_recv, i)

    def dense_copy(i):
        return pltpu.make_async_remote_copy(
            src_ref=dense_out.at[pl.ds(i * rows, rows)],
            dst_ref=dense_in.at[pl.ds(i * rows, rows)],
            send_sem=dense_send.at[i],
            recv_sem=dense_recv.at[i],
            device_id={"mesh": across},
            device_id_type=MESH,
        )

    def theirs(i):
        return acc[pl.ds(pl.multiple_of(other * half + i * rows, rows), rows), :]

    def ours(i):
        return acc[pl.ds(pl.multiple_of(core * half + i * rows, rows), rows), :]

    sums(0)
    if relay:
        for i in range(pieces):
            far_leaving[pl.ds(i * rows, rows), :] = theirs(i).astype(jnp.bfloat16)
            far_copy(i).start()
        for i in range(pieces):
            far_copy(i).wait_recv()
            dense_out[pl.ds(i * rows, rows), :] = (
                ours(i) + far_arrived[pl.ds(i * rows, rows), :].astype(jnp.float32)
            ).astype(jnp.bfloat16)
            dense_copy(i).start()
        sums(1)
    for i in range(pieces):
        leaving[pl.ds(i * rows, rows), :] = theirs(i).astype(jnp.bfloat16)
        half_copy(i).start()
    for i in range(pieces):
        half_copy(i).wait_recv()
        total = ours(i) + arrived[pl.ds(i * rows, rows), :].astype(jnp.float32)
        if relay:
            dense_copy(i).wait_recv()
            total += dense_in[pl.ds(i * rows, rows), :].astype(jnp.float32)
        summed = jnp.dot(
            total.astype(jnp.bfloat16), w_mix[...], preferred_element_type=jnp.float32
        )
        scale = lax.rsqrt(jnp.mean(summed * summed, axis=1, keepdims=True) + 1e-06)
        normed = (summed * scale).astype(jnp.bfloat16)
        inner = silu(jnp.dot(normed, w_in[...], preferred_element_type=jnp.float32))
        out[pl.ds(i * rows, rows), :] = (
            summed
            + jnp.dot(inner.astype(jnp.bfloat16), w_out[...], preferred_element_type=jnp.float32)
        ).astype(out.dtype)
    for i in range(pieces):
        half_copy(i).wait_send()
        if relay:
            far_copy(i).wait_send()
            dense_copy(i).wait_send()
    for f in range(parts):

        def end_rank(j, carry):
            def end_one(t, c):
                entry_copy(f, j, lax.rem(place_in + t, n_part)).wait_send()
                return c

            return lax.fori_loop(1, n_part, end_one, carry)

        def end_word(t, carry):
            word_copy(f, lax.rem(place_in + t, n_part)).wait_send()
            return carry

        lax.fori_loop(0, cap, end_rank, 0)
        lax.fori_loop(1, n_part, end_word, 0)


def main(relay, foot, cap, source, obs, edges, words, w_embed, w_mix, w_in, w_out, n_inst):
    n_mesh = words.shape[0]
    _, obs_n, feats = obs.shape
    width = w_mix.shape[0]
    half = NODE_PART // n_inst
    parts = 2 if relay else 1
    n_part = n_mesh // parts
    unit = min(8, cap * n_part)
    pieces = 4
    bf16 = jnp.bfloat16
    entry = (2, obs_n, feats)
    half_rows = pltpu.VMEM((half, width), bf16)
    return pl.pallas_call(
        functools.partial(main_kernel, relay, foot),
        out_shape=jax.ShapeDtypeStruct((half, width), bf16),
        in_specs=[pl.BlockSpec(memory_space=SMEM)] + [pl.BlockSpec(memory_space=VMEM)] * 7,
        out_specs=pl.BlockSpec(memory_space=VMEM),
        scratch_shapes=[
            pltpu.VMEM((parts, cap, n_part) + entry, bf16),
            pltpu.VMEM((parts, cap, n_part) + entry, bf16),
            pltpu.VMEM((parts, n_part) + words.shape[1:], jnp.int32),
            pltpu.VMEM((NODE_PART, width), jnp.float32),
            pltpu.VMEM((unit * obs_n, w_embed.shape[0]), bf16),
            pltpu.VMEM((unit * obs_n, width), bf16),
            pltpu.VMEM((512, unit * obs_n), bf16),
        ]
        + [half_rows] * 6
        + [pltpu.SemaphoreType.DMA((parts, cap, n_part))] * 2
        + [pltpu.SemaphoreType.DMA((parts, n_part))] * 2
        + [pltpu.SemaphoreType.DMA((pieces,))] * 6,
        compiler_params=pltpu.CompilerParams(
            collective_id=0, has_side_effects=True, vmem_limit_bytes=LIMIT
        ),
    )(source, obs, edges, words, w_embed, w_mix, w_in, w_out)


def per_device(
    observations, instrument, routes, offsets, edges, w_embed, w_mix, w_node_in, w_node_out
):
    n_mesh = lax.axis_size("mesh")
    n_inst = lax.axis_size("inst")
    blocks, obs_n, feats = observations.shape
    foot = routes.shape[1]
    tile_n = edges.shape[3]
    cap = max(2, 2 * blocks * foot // n_mesh)
    slots = n_mesh * cap
    entries = blocks * foot
    dest = routes.reshape(entries)
    index = jnp.arange(entries, dtype=jnp.int32)
    same = (dest[:, None] == dest[None, :]) & (index[None, :] < index[:, None])
    rank = jnp.sum(same.astype(jnp.int32), axis=1)
    position = rank * n_mesh + dest
    words = offsets.reshape(entries) + NODE_PART * jnp.repeat(instrument, foot) + 4 * NODE_PART
    hit = position[None, :] == jnp.arange(slots, dtype=jnp.int32)[:, None]
    source = jnp.sum(jnp.where(hit, index[None, :], 0), axis=1)
    meta = jnp.sum(jnp.where(hit, words[None, :], 0), axis=1)
    by_dest = jnp.pad(meta.reshape(cap, n_mesh).T, ((0, 0), (0, max(8, cap) - cap)))
    spread = jnp.broadcast_to(by_dest[:, :, None], by_dest.shape + (feats,))
    return main(
        RELAY, foot, cap, source, observations, edges.reshape(entries, obs_n, tile_n), spread,
        w_embed.reshape(-1, w_embed.shape[2]), w_mix, w_node_in, w_node_out, n_inst,
    )


def solution(mesh):
    return jax.shard_map(
        per_device,
        mesh=mesh,
        in_specs=(
            P(("groups", "mesh", "inst"), None, None),
            P(("groups", "mesh", "inst")),
            P(("groups", "mesh", "inst"), None),
            P(("groups", "mesh", "inst"), None),
            P(("groups", "mesh", "inst"), None, None, None),
            P(),
            P(),
            P(),
            P(),
        ),
        out_specs=P(("groups", "mesh", "inst"), None),
        check_vma=False,
    )
```

```python
import functools

import jax
import jax.numpy as jnp
from jax import lax
from jax.experimental import pallas as pl
from jax.experimental.pallas import tpu as pltpu
from jax.sharding import PartitionSpec as P

NODE_PART = 2048
ANY = pl.ANY
VMEM = pltpu.VMEM
SMEM = pltpu.SMEM
MESH = pl.DeviceIdType.MESH
LIMIT = 58 * 1024 * 1024
RELAY = True


def silu(v):
    return 0.5 * v * (1.0 + jnp.tanh(0.5 * v))


def main_kernel(
    relay, foot, source, obs_at, edges_at, words, w_embed_at, w_mix_at, w_in_at, w_out_at, out,
    obs, edges, w_embed, w_mix, w_in, w_out, load_sem, packed, got, got_words, acc, kinds_obs, first, placed, leaving, arrived,
    far_leaving, far_arrived, dense_out, dense_in,
    send_sem, recv_sem, word_send, word_recv, half_send, half_recv,
    far_send, far_recv, dense_send, dense_recv,
):
    parts, cap, n_part = got.shape[0], got.shape[1], got.shape[2]
    n_mesh = parts * n_part
    tile_n, feats = got.shape[4], got.shape[5]
    n_kinds = w_embed.shape[0] // feats
    unit = kinds_obs.shape[0] // tile_n
    half = out.shape[0]
    pieces = half_send.shape[0]
    rows = half // pieces
    me = lax.axis_index("mesh")
    part = me // n_part
    place_in = lax.rem(me, n_part)
    across = lax.rem(me + n_part, n_mesh)
    core = lax.axis_index("inst")
    other = 1 - core

    def device(k):
        return part * n_part + k

    def dest(f, k):
        return lax.rem(part + parts - 1 - f, parts) * n_part + k

    loads = [
        pltpu.make_async_copy(src, dst, load_sem.at[i])
        for i, (src, dst) in enumerate(
            [(obs_at, obs), (edges_at, edges), (w_embed_at, w_embed), (w_mix_at, w_mix),
             (w_in_at, w_in), (w_out_at, w_out)]
        )
    ]
    for load in loads:
        load.start()

    barrier = pltpu.get_barrier_semaphore()

    def greet(t, carry):
        to = device(lax.rem(place_in + t, n_part))
        pl.semaphore_signal(barrier, inc=1, device_id={"mesh": to}, device_id_type=MESH)
        return carry

    lax.fori_loop(1, n_part, greet, 0)
    if relay:
        pl.semaphore_signal(barrier, inc=1, device_id={"mesh": across}, device_id_type=MESH)
    pl.semaphore_signal(barrier, inc=1, device_id={"inst": other}, device_id_type=MESH)

    def pack(f, j):
        def one(k, carry):
            entry = source[j * n_mesh + dest(f, k)]
            packed[f, j, k, 0] = obs[entry // foot]
            packed[f, j, k, 1] = edges[entry]
            return carry

        lax.fori_loop(0, n_part, one, 0)

    def entry_copy(f, j, k):
        return pltpu.make_async_remote_copy(
            src_ref=packed.at[f, j, k],
            dst_ref=got.at[f, j, place_in],
            send_sem=send_sem.at[f, j, k],
            recv_sem=recv_sem.at[f, j, place_in],
            device_id={"mesh": device(k)},
            device_id_type=MESH,
        )

    def word_copy(f, k):
        return pltpu.make_async_remote_copy(
            src_ref=words.at[dest(f, k)],
            dst_ref=got_words.at[f, place_in],
            send_sem=word_send.at[f, k],
            recv_sem=word_recv.at[f, place_in],
            device_id={"mesh": device(k)},
            device_id_type=MESH,
        )

    loads[0].wait()
    loads[1].wait()
    pack(0, 0)
    pl.semaphore_wait(barrier, n_part + (1 if relay else 0))
    for f in range(parts):
        pltpu.make_async_copy(
            words.at[dest(f, place_in)], got_words.at[f, place_in], word_recv.at[f, place_in]
        ).start()

        def start_word(t, carry):
            word_copy(f, lax.rem(place_in + t, n_part)).start()
            return carry

        lax.fori_loop(1, n_part, start_word, 0)

    for f in range(parts):

        def start_rank(j, carry):
            if f == 0:

                @pl.when(j > 0)
                def _():
                    pack(f, j)

            else:
                pack(f, j)
            pltpu.make_async_copy(
                packed.at[f, j, place_in], got.at[f, j, place_in], recv_sem.at[f, j, place_in]
            ).start()

            def start_one(t, c):
                entry_copy(f, j, lax.rem(place_in + t, n_part)).start()
                return c

            return lax.fori_loop(1, n_part, start_one, carry)

        lax.fori_loop(0, cap, start_rank, 0)

    for f in range(parts):

        def wait_word(s, carry):
            pltpu.make_async_copy(words.at[s], got_words.at[f, s], word_recv.at[f, s]).wait()
            return carry

        lax.fori_loop(0, n_part, wait_word, 0)

    place = lax.broadcasted_iota(jnp.int32, (tile_n, tile_n), 0)
    lane = lax.broadcasted_iota(jnp.int32, (tile_n, tile_n), 1)
    group_rows = placed.shape[0]
    tiles = group_rows // tile_n

    def sums(f):
        acc[...] = jnp.zeros_like(acc)

        def work(u, carry):
            owners = []
            turned = []
            for s in range(unit):
                slot = u * unit + s
                j = slot // n_part
                src = lax.rem(slot, n_part)
                pltpu.make_async_copy(
                    packed.at[f, j, src], got.at[f, j, src], recv_sem.at[f, j, src]
                ).wait()
                word = got_words[f, src, pl.ds(j, 1), :]
                kind = (word // NODE_PART) % 4
                x = got[f, j, src, 0]
                for k in range(n_kinds):
                    mask = jnp.broadcast_to((kind == k).astype(jnp.float32), (tile_n, feats))
                    kinds_obs[s * tile_n : (s + 1) * tile_n, k * feats : (k + 1) * feats] = (
                        x * mask.astype(jnp.bfloat16)
                    )
                begin = word % NODE_PART
                turn = begin % tile_n
                q = jnp.where(word >= 4 * NODE_PART, begin // tile_n, -100)
                owner = q + jnp.where(place < turn, 1, 0)
                owners.append(owner.astype(jnp.float32).astype(jnp.bfloat16))
                moves = jnp.where((lane + turn) % tile_n == place, 1.0, 0.0).astype(jnp.bfloat16)
                turned.append(
                    lax.dot_general(
                        moves, got[f, j, src, 1], (((1,), (1,)), ((), ())),
                        preferred_element_type=jnp.float32,
                    ).astype(jnp.bfloat16)
                )
            first[...] = silu(
                jnp.dot(kinds_obs[...], w_embed[...], preferred_element_type=jnp.float32)
            ).astype(jnp.bfloat16)
            for g in range(NODE_PART // group_rows):
                for s in range(unit):
                    for n in range(tiles):
                        here = owners[s] == jnp.bfloat16(g * tiles + n)
                        placed[n * tile_n : (n + 1) * tile_n, s * tile_n : (s + 1) * tile_n] = (
                            jnp.where(here, turned[s], jnp.bfloat16(0))
                        )
                acc[g * group_rows : (g + 1) * group_rows, :] += jnp.dot(
                    placed[...], first[...], preferred_element_type=jnp.float32
                )
            return carry

        lax.fori_loop(0, cap * n_part // unit, work, 0)

    def to_core(src, dst, sent, come, i):
        return pltpu.make_async_remote_copy(
            src_ref=src.at[pl.ds(i * rows, rows)],
            dst_ref=dst.at[pl.ds(i * rows, rows)],
            send_sem=sent.at[i],
            recv_sem=come.at[i],
            device_id={"inst": other},
            device_id_type=MESH,
        )

    def far_copy(i):
        return to_core(far_leaving, far_arrived, far_send, far_recv, i)

    def half_copy(i):
        return to_core(leaving, arrived, half_send, half_recv, i)

    def dense_copy(i):
        return pltpu.make_async_remote_copy(
            src_ref=dense_out.at[pl.ds(i * rows, rows)],
            dst_ref=dense_in.at[pl.ds(i * rows, rows)],
            send_sem=dense_send.at[i],
            recv_sem=dense_recv.at[i],
            device_id={"mesh": across},
            device_id_type=MESH,
        )

    def theirs(i):
        return acc[pl.ds(pl.multiple_of(other * half + i * rows, rows), rows), :]

    def ours(i):
        return acc[pl.ds(pl.multiple_of(core * half + i * rows, rows), rows), :]

    for load in loads[2:]:
        load.wait()
    sums(0)
    if relay:
        for i in range(pieces):
            far_leaving[pl.ds(i * rows, rows), :] = theirs(i).astype(jnp.bfloat16)
            far_copy(i).start()
        for i in range(pieces):
            far_copy(i).wait_recv()
            dense_out[pl.ds(i * rows, rows), :] = (
                ours(i) + far_arrived[pl.ds(i * rows, rows), :].astype(jnp.float32)
            ).astype(jnp.bfloat16)
            dense_copy(i).start()
        sums(1)
    for i in range(pieces):
        leaving[pl.ds(i * rows, rows), :] = theirs(i).astype(jnp.bfloat16)
        half_copy(i).start()
    for f in range(parts):

        def end_rank(j, carry):
            def end_one(t, c):
                entry_copy(f, j, lax.rem(place_in + t, n_part)).wait_send()
                return c

            return lax.fori_loop(1, n_part, end_one, carry)

        def end_word(t, carry):
            word_copy(f, lax.rem(place_in + t, n_part)).wait_send()
            return carry

        lax.fori_loop(0, cap, end_rank, 0)
        lax.fori_loop(1, n_part, end_word, 0)
    for i in range(pieces):
        half_copy(i).wait_recv()
        total = ours(i) + arrived[pl.ds(i * rows, rows), :].astype(jnp.float32)
        if relay:
            dense_copy(i).wait_recv()
            total += dense_in[pl.ds(i * rows, rows), :].astype(jnp.float32)
        summed = jnp.dot(
            total.astype(jnp.bfloat16), w_mix[...], preferred_element_type=jnp.float32
        )
        scale = lax.rsqrt(jnp.mean(summed * summed, axis=1, keepdims=True) + 1e-06)
        normed = (summed * scale).astype(jnp.bfloat16)
        inner = silu(jnp.dot(normed, w_in[...], preferred_element_type=jnp.float32))
        out[pl.ds(i * rows, rows), :] = (
            summed
            + jnp.dot(inner.astype(jnp.bfloat16), w_out[...], preferred_element_type=jnp.float32)
        ).astype(out.dtype)
    for i in range(pieces):
        half_copy(i).wait_send()
        if relay:
            far_copy(i).wait_send()
            dense_copy(i).wait_send()


def main(relay, foot, cap, source, obs, edges, words, w_embed, w_mix, w_in, w_out, n_inst):
    n_mesh = words.shape[0]
    _, obs_n, feats = obs.shape
    width = w_mix.shape[0]
    half = NODE_PART // n_inst
    parts = 2 if relay else 1
    n_part = n_mesh // parts
    unit = min(4, cap * n_part)
    pieces = 8
    bf16 = jnp.bfloat16
    entry = (2, obs_n, feats)
    half_rows = pltpu.VMEM((half, width), bf16)
    return pl.pallas_call(
        functools.partial(main_kernel, relay, foot),
        out_shape=jax.ShapeDtypeStruct((half, width), bf16),
        in_specs=[pl.BlockSpec(memory_space=SMEM)]
        + [pl.BlockSpec(memory_space=ANY)] * 2
        + [pl.BlockSpec(memory_space=VMEM)]
        + [pl.BlockSpec(memory_space=ANY)] * 4,
        out_specs=pl.BlockSpec(memory_space=VMEM),
        scratch_shapes=[pltpu.VMEM(a.shape, bf16) for a in (obs, edges, w_embed, w_mix, w_in, w_out)]
        + [
            pltpu.SemaphoreType.DMA((6,)),
            pltpu.VMEM((parts, cap, n_part) + entry, bf16),
            pltpu.VMEM((parts, cap, n_part) + entry, bf16),
            pltpu.VMEM((parts, n_part) + words.shape[1:], jnp.int32),
            pltpu.VMEM((NODE_PART, width), jnp.float32),
            pltpu.VMEM((unit * obs_n, w_embed.shape[0]), bf16),
            pltpu.VMEM((unit * obs_n, width), bf16),
            pltpu.VMEM((512, unit * obs_n), bf16),
        ]
        + [half_rows] * 6
        + [pltpu.SemaphoreType.DMA((parts, cap, n_part))] * 2
        + [pltpu.SemaphoreType.DMA((parts, n_part))] * 2
        + [pltpu.SemaphoreType.DMA((pieces,))] * 6,
        compiler_params=pltpu.CompilerParams(
            collective_id=0, has_side_effects=True, vmem_limit_bytes=LIMIT
        ),
    )(source, obs, edges, words, w_embed, w_mix, w_in, w_out)


def per_device(
    observations, instrument, routes, offsets, edges, w_embed, w_mix, w_node_in, w_node_out
):
    n_mesh = lax.axis_size("mesh")
    n_inst = lax.axis_size("inst")
    blocks, obs_n, feats = observations.shape
    foot = routes.shape[1]
    tile_n = edges.shape[3]
    cap = max(2, 2 * blocks * foot // n_mesh)
    slots = n_mesh * cap
    entries = blocks * foot
    dest = routes.reshape(entries)
    index = jnp.arange(entries, dtype=jnp.int32)
    same = (dest[:, None] == dest[None, :]) & (index[None, :] < index[:, None])
    rank = jnp.sum(same.astype(jnp.int32), axis=1)
    position = rank * n_mesh + dest
    words = offsets.reshape(entries) + NODE_PART * jnp.repeat(instrument, foot) + 4 * NODE_PART
    hit = position[None, :] == jnp.arange(slots, dtype=jnp.int32)[:, None]
    source = jnp.sum(jnp.where(hit, index[None, :], 0), axis=1)
    meta = jnp.sum(jnp.where(hit, words[None, :], 0), axis=1)
    by_dest = jnp.pad(meta.reshape(cap, n_mesh).T, ((0, 0), (0, max(8, cap) - cap)))
    spread = jnp.broadcast_to(by_dest[:, :, None], by_dest.shape + (feats,))
    return main(
        RELAY, foot, cap, source, observations, edges.reshape(entries, obs_n, tile_n), spread,
        w_embed.reshape(-1, w_embed.shape[2]), w_mix, w_node_in, w_node_out, n_inst,
    )


def solution(mesh):
    return jax.shard_map(
        per_device,
        mesh=mesh,
        in_specs=(
            P(("groups", "mesh", "inst"), None, None),
            P(("groups", "mesh", "inst")),
            P(("groups", "mesh", "inst"), None),
            P(("groups", "mesh", "inst"), None),
            P(("groups", "mesh", "inst"), None, None, None),
            P(),
            P(),
            P(),
            P(),
        ),
        out_specs=P(("groups", "mesh", "inst"), None),
        check_vma=False,
    )
```

```python
import functools

import jax
import jax.numpy as jnp
from jax import lax
from jax.experimental import pallas as pl
from jax.experimental.pallas import tpu as pltpu
from jax.sharding import PartitionSpec as P

NODE_PART = 2048
ANY = pl.ANY
VMEM = pltpu.VMEM
SMEM = pltpu.SMEM
MESH = pl.DeviceIdType.MESH
LIMIT = 48 * 1024 * 1024
RELAY = True


def silu(v):
    return 0.5 * v * (1.0 + jnp.tanh(0.5 * v))


def main_kernel(
    relay, foot, source, obs_at, edges_at, words, w_embed_at, w_mix_at, w_in_at, w_out_at, out,
    obs, edges, w_embed, w_mix, w_in, w_out, load_sem, packed, got, got_words, acc, kinds_obs, first, placed, leaving, arrived,
    far_leaving, far_arrived, dense_out, dense_in,
    send_sem, recv_sem, word_send, word_recv, half_send, half_recv,
    far_send, far_recv, dense_send, dense_recv,
):
    parts, cap, n_part = got.shape[0], got.shape[1], got.shape[2]
    n_mesh = parts * n_part
    tile_n, feats = got.shape[4], got.shape[5]
    n_kinds = w_embed.shape[0] // feats
    unit = kinds_obs.shape[0] // tile_n
    half = out.shape[0]
    pieces = half_send.shape[0]
    rows = half // pieces
    me = lax.axis_index("mesh")
    part = me // n_part
    place_in = lax.rem(me, n_part)
    across = lax.rem(me + n_part, n_mesh)
    core = lax.axis_index("inst")
    other = 1 - core

    def device(k):
        return part * n_part + k

    def dest(f, k):
        return lax.rem(part + parts - 1 - f, parts) * n_part + k

    loads = [
        pltpu.make_async_copy(src, dst, load_sem.at[i])
        for i, (src, dst) in enumerate(
            [(obs_at, obs), (edges_at, edges), (w_embed_at, w_embed), (w_mix_at, w_mix),
             (w_in_at, w_in), (w_out_at, w_out)]
        )
    ]
    for load in loads:
        load.start()

    barrier = pltpu.get_barrier_semaphore()

    def greet(t, carry):
        to = device(lax.rem(place_in + t, n_part))
        pl.semaphore_signal(barrier, inc=1, device_id={"mesh": to}, device_id_type=MESH)
        return carry

    lax.fori_loop(1, n_part, greet, 0)
    if relay:
        pl.semaphore_signal(barrier, inc=1, device_id={"mesh": across}, device_id_type=MESH)
    pl.semaphore_signal(barrier, inc=1, device_id={"inst": other}, device_id_type=MESH)

    def pack(f, j):
        def one(k, carry):
            entry = source[j * n_mesh + dest(f, k)]
            packed[f, j, k, 0] = obs[entry // foot]
            packed[f, j, k, 1] = edges[entry]
            return carry

        lax.fori_loop(0, n_part, one, 0)

    def entry_copy(f, j, k):
        return pltpu.make_async_remote_copy(
            src_ref=packed.at[f, j, k],
            dst_ref=got.at[f, j, place_in],
            send_sem=send_sem.at[f, j, k],
            recv_sem=recv_sem.at[f, j, place_in],
            device_id={"mesh": device(k)},
            device_id_type=MESH,
        )

    def word_copy(f, k):
        return pltpu.make_async_remote_copy(
            src_ref=words.at[dest(f, k)],
            dst_ref=got_words.at[f, place_in],
            send_sem=word_send.at[f, k],
            recv_sem=word_recv.at[f, place_in],
            device_id={"mesh": device(k)},
            device_id_type=MESH,
        )

    loads[0].wait()
    loads[1].wait()
    pack(0, 0)
    pl.semaphore_wait(barrier, n_part + (1 if relay else 0))
    for f in range(parts):
        pltpu.make_async_copy(
            words.at[dest(f, place_in)], got_words.at[f, place_in], word_recv.at[f, place_in]
        ).start()

        def start_word(t, carry):
            word_copy(f, lax.rem(place_in + t, n_part)).start()
            return carry

        lax.fori_loop(1, n_part, start_word, 0)

    for f in range(parts):

        def start_rank(j, carry):
            if f == 0:

                @pl.when(j > 0)
                def _():
                    pack(f, j)

            else:
                pack(f, j)
            pltpu.make_async_copy(
                packed.at[f, j, place_in], got.at[f, j, place_in], recv_sem.at[f, j, place_in]
            ).start()

            def start_one(t, c):
                entry_copy(f, j, lax.rem(place_in + t, n_part)).start()
                return c

            return lax.fori_loop(1, n_part, start_one, carry)

        lax.fori_loop(0, cap, start_rank, 0)

    for f in range(parts):

        def wait_word(s, carry):
            pltpu.make_async_copy(words.at[s], got_words.at[f, s], word_recv.at[f, s]).wait()
            return carry

        lax.fori_loop(0, n_part, wait_word, 0)

    place = lax.broadcasted_iota(jnp.int32, (tile_n, tile_n), 0)
    lane = lax.broadcasted_iota(jnp.int32, (tile_n, tile_n), 1)
    group_rows = placed.shape[0]
    tiles = group_rows // tile_n

    def sums(f):
        acc[...] = jnp.zeros_like(acc)

        def work(u, carry):
            owners = []
            turned = []
            for s in range(unit):
                slot = u * unit + s
                j = slot // n_part
                src = lax.rem(slot, n_part)
                pltpu.make_async_copy(
                    packed.at[f, j, src], got.at[f, j, src], recv_sem.at[f, j, src]
                ).wait()
                word = got_words[f, src, pl.ds(j, 1), :]
                kind = (word // NODE_PART) % 4
                x = got[f, j, src, 0]
                for k in range(n_kinds):
                    mask = jnp.broadcast_to((kind == k).astype(jnp.float32), (tile_n, feats))
                    kinds_obs[s * tile_n : (s + 1) * tile_n, k * feats : (k + 1) * feats] = (
                        x * mask.astype(jnp.bfloat16)
                    )
                begin = word % NODE_PART
                turn = begin % tile_n
                q = jnp.where(word >= 4 * NODE_PART, begin // tile_n, -100)
                owner = q + jnp.where(place < turn, 1, 0)
                owners.append(owner.astype(jnp.float32).astype(jnp.bfloat16))
                moves = jnp.where((lane + turn) % tile_n == place, 1.0, 0.0).astype(jnp.bfloat16)
                turned.append(
                    lax.dot_general(
                        moves, got[f, j, src, 1], (((1,), (1,)), ((), ())),
                        preferred_element_type=jnp.float32,
                    ).astype(jnp.bfloat16)
                )
            first[...] = silu(
                jnp.dot(kinds_obs[...], w_embed[...], preferred_element_type=jnp.float32)
            ).astype(jnp.bfloat16)
            for g in range(NODE_PART // group_rows):
                for s in range(unit):
                    for n in range(tiles):
                        here = owners[s] == jnp.bfloat16(g * tiles + n)
                        placed[n * tile_n : (n + 1) * tile_n, s * tile_n : (s + 1) * tile_n] = (
                            jnp.where(here, turned[s], jnp.bfloat16(0))
                        )
                acc[g * group_rows : (g + 1) * group_rows, :] += jnp.dot(
                    placed[...], first[...], preferred_element_type=jnp.float32
                )
            return carry

        lax.fori_loop(0, cap * n_part // unit, work, 0)

    def to_core(src, dst, sent, come, i):
        return pltpu.make_async_remote_copy(
            src_ref=src.at[pl.ds(i * rows, rows)],
            dst_ref=dst.at[pl.ds(i * rows, rows)],
            send_sem=sent.at[i],
            recv_sem=come.at[i],
            device_id={"inst": other},
            device_id_type=MESH,
        )

    def far_copy(i):
        return to_core(far_leaving, far_arrived, far_send, far_recv, i)

    def half_copy(i):
        return to_core(leaving, arrived, half_send, half_recv, i)

    def dense_copy(i):
        return pltpu.make_async_remote_copy(
            src_ref=dense_out.at[pl.ds(i * rows, rows)],
            dst_ref=dense_in.at[pl.ds(i * rows, rows)],
            send_sem=dense_send.at[i],
            recv_sem=dense_recv.at[i],
            device_id={"mesh": across},
            device_id_type=MESH,
        )

    def theirs(i):
        return acc[pl.ds(pl.multiple_of(other * half + i * rows, rows), rows), :]

    def ours(i):
        return acc[pl.ds(pl.multiple_of(core * half + i * rows, rows), rows), :]

    for load in loads[2:]:
        load.wait()
    sums(0)
    if relay:
        for i in range(pieces):
            far_leaving[pl.ds(i * rows, rows), :] = theirs(i).astype(jnp.bfloat16)
            far_copy(i).start()
        for i in range(pieces):
            far_copy(i).wait_recv()
            dense_out[pl.ds(i * rows, rows), :] = (
                ours(i) + far_arrived[pl.ds(i * rows, rows), :].astype(jnp.float32)
            ).astype(jnp.bfloat16)
            dense_copy(i).start()
        sums(1)
    for i in range(pieces):
        leaving[pl.ds(i * rows, rows), :] = theirs(i).astype(jnp.bfloat16)
        half_copy(i).start()
    for f in range(parts):

        def end_rank(j, carry):
            def end_one(t, c):
                entry_copy(f, j, lax.rem(place_in + t, n_part)).wait_send()
                return c

            return lax.fori_loop(1, n_part, end_one, carry)

        def end_word(t, carry):
            word_copy(f, lax.rem(place_in + t, n_part)).wait_send()
            return carry

        lax.fori_loop(0, cap, end_rank, 0)
        lax.fori_loop(1, n_part, end_word, 0)
    for i in range(pieces):
        half_copy(i).wait_recv()
        total = ours(i) + arrived[pl.ds(i * rows, rows), :].astype(jnp.float32)
        if relay:
            dense_copy(i).wait_recv()
            total += dense_in[pl.ds(i * rows, rows), :].astype(jnp.float32)
        summed = jnp.dot(
            total.astype(jnp.bfloat16), w_mix[...], preferred_element_type=jnp.float32
        )
        scale = lax.rsqrt(jnp.mean(summed * summed, axis=1, keepdims=True) + 1e-06)
        normed = (summed * scale).astype(jnp.bfloat16)
        inner = silu(jnp.dot(normed, w_in[...], preferred_element_type=jnp.float32))
        out[pl.ds(i * rows, rows), :] = (
            summed
            + jnp.dot(inner.astype(jnp.bfloat16), w_out[...], preferred_element_type=jnp.float32)
        ).astype(out.dtype)
    for i in range(pieces):
        half_copy(i).wait_send()
        if relay:
            far_copy(i).wait_send()
            dense_copy(i).wait_send()


def main(relay, foot, cap, source, obs, edges, words, w_embed, w_mix, w_in, w_out, n_inst):
    n_mesh = words.shape[0]
    _, obs_n, feats = obs.shape
    width = w_mix.shape[0]
    half = NODE_PART // n_inst
    parts = 2 if relay else 1
    n_part = n_mesh // parts
    unit = min(4, cap * n_part)
    pieces = 8
    bf16 = jnp.bfloat16
    entry = (2, obs_n, feats)
    half_rows = pltpu.VMEM((half, width), bf16)
    return pl.pallas_call(
        functools.partial(main_kernel, relay, foot),
        out_shape=jax.ShapeDtypeStruct((half, width), bf16),
        in_specs=[pl.BlockSpec(memory_space=SMEM)]
        + [pl.BlockSpec(memory_space=ANY)] * 2
        + [pl.BlockSpec(memory_space=VMEM)]
        + [pl.BlockSpec(memory_space=ANY)] * 4,
        out_specs=pl.BlockSpec(memory_space=VMEM),
        scratch_shapes=[pltpu.VMEM(a.shape, bf16) for a in (obs, edges, w_embed, w_mix, w_in, w_out)]
        + [
            pltpu.SemaphoreType.DMA((6,)),
            pltpu.VMEM((parts, cap, n_part) + entry, bf16),
            pltpu.VMEM((parts, cap, n_part) + entry, bf16),
            pltpu.VMEM((parts, n_part) + words.shape[1:], jnp.int32),
            pltpu.VMEM((NODE_PART, width), jnp.float32),
            pltpu.VMEM((unit * obs_n, w_embed.shape[0]), bf16),
            pltpu.VMEM((unit * obs_n, width), bf16),
            pltpu.VMEM((512, unit * obs_n), bf16),
        ]
        + [half_rows] * 6
        + [pltpu.SemaphoreType.DMA((parts, cap, n_part))] * 2
        + [pltpu.SemaphoreType.DMA((parts, n_part))] * 2
        + [pltpu.SemaphoreType.DMA((pieces,))] * 6,
        compiler_params=pltpu.CompilerParams(
            collective_id=0, has_side_effects=True, vmem_limit_bytes=LIMIT
        ),
    )(source, obs, edges, words, w_embed, w_mix, w_in, w_out)


def per_device(
    observations, instrument, routes, offsets, edges, w_embed, w_mix, w_node_in, w_node_out
):
    n_mesh = lax.axis_size("mesh")
    n_inst = lax.axis_size("inst")
    blocks, obs_n, feats = observations.shape
    foot = routes.shape[1]
    tile_n = edges.shape[3]
    cap = max(2, 2 * blocks * foot // n_mesh)
    slots = n_mesh * cap
    entries = blocks * foot
    dest = routes.reshape(entries)
    index = jnp.arange(entries, dtype=jnp.int32)
    same = (dest[:, None] == dest[None, :]) & (index[None, :] < index[:, None])
    rank = jnp.sum(same.astype(jnp.int32), axis=1)
    position = rank * n_mesh + dest
    words = offsets.reshape(entries) + NODE_PART * jnp.repeat(instrument, foot) + 4 * NODE_PART
    hit = position[None, :] == jnp.arange(slots, dtype=jnp.int32)[:, None]
    source = jnp.sum(jnp.where(hit, index[None, :], 0), axis=1)
    meta = jnp.sum(jnp.where(hit, words[None, :], 0), axis=1)
    by_dest = jnp.pad(meta.reshape(cap, n_mesh).T, ((0, 0), (0, max(8, cap) - cap)))
    spread = jnp.broadcast_to(by_dest[:, :, None], by_dest.shape + (feats,))
    return main(
        RELAY, foot, cap, source, observations, edges.reshape(entries, obs_n, tile_n), spread,
        w_embed.reshape(-1, w_embed.shape[2]), w_mix, w_node_in, w_node_out, n_inst,
    )


def solution(mesh):
    return jax.shard_map(
        per_device,
        mesh=mesh,
        in_specs=(
            P(("groups", "mesh", "inst"), None, None),
            P(("groups", "mesh", "inst")),
            P(("groups", "mesh", "inst"), None),
            P(("groups", "mesh", "inst"), None),
            P(("groups", "mesh", "inst"), None, None, None),
            P(),
            P(),
            P(),
            P(),
        ),
        out_specs=P(("groups", "mesh", "inst"), None),
        check_vma=False,
    )
```
